32 devices in a mesh: span: 4 (over y, x), tile: 8 (over z, core).
Axes of the slice: x: 2, y: 2, z: 4, core: 2. Of those that a mesh axis runs over, the one named last changes fastest.
Arguments:
- clean_latents: bfloat16 [4, 2, 32, 2560], P('span', None, 'tile'), may hold values from -6 to 6
- noise_draws: bfloat16 [4, 2, 32, 2560], P('span', None, 'tile'), may hold values from -6 to 6
- noise_level: float32 [4], P('span'), may hold values from 0.3 to 3
- memory_bank: bfloat16 [128, 32, 2560], P('span', 'tile'), may hold values from -6 to 6
- memory_index: int32 [4, 16], P('span'), may hold values from 0 to 127, as said below
- stem_weight: bfloat16 [16, 512], replicated, may hold values from -1.5 to 1.5
- memory_weight: bfloat16 [256, 512], replicated, may hold values from -0.375 to 0.375
- conv_weight: bfloat16 [2, 3, 3, 3, 32, 512], replicated, may hold values from -0.21875 to 0.21875
- norm_gain: float32 [2, 512], replicated, may hold values from 0.1 to 1.9
- head_weight: bfloat16 [512, 16], replicated, may hold values from -0.25 to 0.25
Outputs:
- prediction: bfloat16 [4, 2, 32, 2560], P('span', None, 'tile')
The draws below stay inside these ranges and needn't reach their ends.
Inputs may be any that keep to these rules, and one draw needn't show every extreme that they name: `memory_index`: entry = owner span times 32 plus a frame of that owner. No row names more than 4 entries of one owner; one owner, the same for all rows, is named exactly 4 times in every row. Entries may repeat.
All inputs are finite; a program needn't handle non-finite values.
Results may differ from the reference program's by a relative error of at most 0.012.
Values may be sent and summed in bfloat16 or wider, within the bound.
A program may use at most 128 MiB of HBM per device.

```python
import math
import jax
import jax.numpy as jnp
from jax import lax

C = 512
CG = 32
LAT = 16
W = 160
FR = 2
CTX = 2
LAYERS = 2
MEMS = 16
CAP = 4
BANK_DEV = 32
SPANS = 4
H = 32


def draw_memory_index(key, part):
    base_key = jax.random.fold_in(key, 11)
    key_hot, key_other, key_local, key_order = jax.random.split(base_key, 4)
    hot_owner = jax.random.randint(key_hot, (), 0, SPANS)
    pool_size = (SPANS - 1) * CAP
    pool = jnp.arange(pool_size, dtype=jnp.int32) // CAP
    pool = pool + (pool >= hot_owner).astype(jnp.int32)
    pool_scores = jax.random.randint(key_other, (SPANS, pool_size), 0, 1 << 20) * pool_size + jnp.arange(pool_size, dtype=jnp.int32)[None, :]
    pool_order = jnp.argsort(pool_scores, axis=1, stable=True)[:, :MEMS - CAP]
    others = pool[pool_order]
    owners = jnp.concatenate([jnp.zeros((SPANS, CAP), jnp.int32) + hot_owner, others], axis=1)
    local_frame = jax.random.randint(key_local, (SPANS, MEMS), 0, BANK_DEV)
    order_scores = jax.random.randint(key_order, (SPANS, MEMS), 0, 1 << 20) * MEMS + jnp.arange(MEMS, dtype=jnp.int32)[None, :]
    slot_order = jnp.argsort(order_scores, axis=1, stable=True)
    frame_ids = owners * BANK_DEV + local_frame
    return jnp.take_along_axis(frame_ids, slot_order, axis=1).astype(jnp.int32)


def level_of(own_key, shape, shards, smallest, high):
    gain, own = 1.0, jax.random.fold_in(own_key, 6)
    for dim, parts in shards:
        steps = jnp.exp(jax.random.uniform(jax.random.fold_in(own, dim), (parts,), jnp.float32, smallest / len(shards), high / len(shards)))
        gain = gain * jnp.repeat(steps, shape[dim] // parts).reshape([-1 if axis == dim else 1 for axis in range(len(shape))])
    return gain


def scatter_about(rng, shape, scale, reach, pieces=(), held_as=jnp.bfloat16):
    gain = level_of(rng, shape, pieces, -0.22, 0.18) if pieces else 1.0
    values = jax.random.normal(rng, shape, jnp.float32) * scale * gain
    return jnp.minimum(jnp.maximum(values, -reach), reach).astype(held_as)


def setup_inputs(seed: int = 0) -> dict:
    keys = jax.random.split(jax.random.key(seed), 11)
    return {
        "clean_latents": scatter_about(keys[0], (SPANS, FR, H, W * LAT), 1.0, 6.0, ((0, 4), (2, 8))),
        "noise_draws": scatter_about(keys[1], (SPANS, FR, H, W * LAT), 1.0, 6.0, ((0, 4), (2, 8))),
        "noise_level": jnp.clip(jnp.exp(math.log(3.0) - 2.3025851 * jax.random.uniform(keys[2], (SPANS,), jnp.float32) ** level_of(keys[2], (SPANS,), ((0, 4),), -0.2, 0.2)), 0.3, 3.0),
        "memory_bank": scatter_about(keys[3], (SPANS * BANK_DEV, H, W * LAT), 1.0, 6.0, ((0, 4), (1, 8))),
        "memory_index": draw_memory_index(jax.random.fold_in(keys[10], 71), 0),
        "stem_weight": scatter_about(keys[5], (LAT, C), LAT ** -0.5, 1.5),
        "memory_weight": scatter_about(keys[6], (MEMS * LAT, C), (MEMS * LAT) ** -0.5, 0.375),
        "conv_weight": scatter_about(keys[7], (LAYERS, 3, 3, 3, CG, C), (27 * CG) ** -0.5, 0.21875),
        "norm_gain": jnp.clip(1.0 + 0.18 * jax.random.normal(keys[8], (LAYERS, C), jnp.float32), 0.1, 1.9),
        "head_weight": scatter_about(keys[9], (C, LAT), C ** -0.5, 0.25),
    }


def normed_silu(hidden, gain_row):
    values = hidden.astype(jnp.float32)
    mean_square = lax.optimization_barrier(jnp.mean(values * values, axis=-1, keepdims=True))
    scaled = values * lax.rsqrt(mean_square + 1e-06) * gain_row.astype(jnp.float32)
    return jax.nn.silu(scaled).astype(jnp.bfloat16)

def causal_conv(active, weight):
    frames, row_count, col_count, channels = active.shape
    group_width = weight.shape[3]
    group_count = channels // group_width
    padded = jnp.pad(active, ((2, 0), (1, 1), (1, 1), (0, 0))).astype(jnp.float32)
    accumulated = jnp.zeros((frames, row_count, col_count, group_count, group_width), jnp.float32)
    for time_tap in range(3):
        for row_tap in range(3):
            for col_tap in range(3):
                window_slice = padded[time_tap:time_tap + frames, row_tap:row_tap + row_count, col_tap:col_tap + col_count]
                window_slice = window_slice.reshape(frames, row_count, col_count, group_count, group_width)
                kernel = weight[time_tap, row_tap, col_tap].astype(jnp.float32).reshape(group_width, group_count, group_width)
                accumulated = accumulated + jnp.einsum('fhwgi,igo->fhwgo', window_slice, kernel)
    return accumulated.reshape(frames, row_count, col_count, channels)

def reference(clean_latents, noise_draws, noise_level, memory_bank, memory_index, stem_weight, memory_weight, conv_weight, norm_gain, head_weight):
    channels = stem_weight.shape[1]
    zero_block = jnp.zeros((1, CTX, H, W * LAT), jnp.bfloat16)
    previous = jnp.concatenate([zero_block, clean_latents[:-1, FR - CTX:]], axis=0)

    def one_span(operands):
        clean_span, noise_span, sigma_value, previous_span, index_row = operands
        noisy = ((clean_span.astype(jnp.float32) + sigma_value * noise_span.astype(jnp.float32)) * lax.rsqrt(1.0 + sigma_value * sigma_value)).astype(jnp.bfloat16)
        sequence = jnp.concatenate([previous_span, noisy], axis=0)
        memory = memory_bank[index_row]
        frames = sequence.shape[0]
        stem_term = jnp.dot(sequence.reshape(frames * H * W, LAT), stem_weight, preferred_element_type=jnp.float32).reshape(frames, H, W, channels)
        stacked = jnp.transpose(memory.reshape(MEMS, H, W, LAT), (1, 2, 0, 3)).reshape(H * W, MEMS * LAT)
        memory_term = jnp.dot(stacked, memory_weight, preferred_element_type=jnp.float32).reshape(H, W, channels)
        hidden = (stem_term + memory_term[None]).astype(jnp.bfloat16)
        for layer_number in range(LAYERS):
            active = normed_silu(hidden, norm_gain[layer_number])
            update = causal_conv(active, conv_weight[layer_number])
            hidden = (hidden.astype(jnp.float32) + update).astype(jnp.bfloat16)
        tail = hidden[CTX:].reshape(-1, channels)
        output = jnp.dot(tail, head_weight, preferred_element_type=jnp.float32).astype(jnp.bfloat16)
        return output.reshape(FR, H, W * LAT)
    return lax.map(one_span, (clean_latents, noise_draws, noise_level, previous, memory_index))
```

```python
import functools

import jax
import jax.numpy as jnp
from jax import lax
from jax.experimental import pallas as pl
from jax.experimental.pallas import tpu as pltpu
from jax.sharding import PartitionSpec as P

CTX = 2
CAP = 4
BLK = 256
CHUNK = 2


def shifted(value, axis, steps):
    count = lax.axis_size(axis)
    first, last = (max(0, -steps), min(count, count - steps))
    return lax.ppermute(value, axis, [(source, source + steps) for source in range(first, last)])


def with_halo(block, sides, width):
    for axis, dim in sides:
        count = lax.axis_size(axis)
        forward = [(i, i + 1) for i in range(count - 1)]
        backward = [(target, source) for source, target in forward]
        low = lax.ppermute(
            lax.slice_in_dim(block, block.shape[dim] - width, None, axis=dim), axis, forward
        )
        high = lax.ppermute(lax.slice_in_dim(block, 0, width, axis=dim), axis, backward)
        block = jnp.concatenate([low, block, high], axis=dim)
    return block


def select_frames(frames, index):
    chosen = index[:, None] == jnp.arange(frames.shape[0], dtype=jnp.int32)[None, :]
    return jnp.einsum(
        "sf,frm->srm",
        chosen.astype(jnp.bfloat16),
        frames,
        preferred_element_type=jnp.float32,
    ).astype(jnp.bfloat16)


def fetch_memory(memory_bank, memory_index):
    wanted = memory_index[0]
    bank_frames, row_count, merged = memory_bank.shape
    span_count = lax.axis_size("span")
    memory_count = wanted.shape[0]
    owner_span = wanted // bank_frames
    local_frame = wanted % bank_frames
    positions = jnp.arange(memory_count, dtype=jnp.int32)
    same_owner = (owner_span[:, None] == owner_span[None, :]) & (
        positions[None, :] < positions[:, None]
    )
    owner_rank = jnp.sum(same_owner.astype(jnp.int32), axis=1)
    reply_slot = owner_span * CAP + owner_rank
    slot_match = jnp.arange(span_count * CAP, dtype=jnp.int32)[:, None] == reply_slot[None, :]
    request = jnp.sum(jnp.where(slot_match, local_frame[None, :] + 1, 0), axis=1) - 1
    request = request.reshape(span_count, CAP)
    incoming = lax.all_to_all(request, "span", split_axis=0, concat_axis=0, tiled=True)
    picked = select_frames(memory_bank, incoming.reshape(-1)).reshape(
        span_count, CAP, row_count, merged
    )
    returned = lax.all_to_all(picked, "span", split_axis=0, concat_axis=0, tiled=True)
    return select_frames(returned.reshape(span_count * CAP, row_count, merged), reply_slot)


def kernel(rows, x_ref, w_ref, cw_ref, gain_ref, head_ref, out_ref, h0, a1, h1, a2, wexp):
    frames = h0.shape[0]
    cols = x_ref.shape[0] // (rows + 4)
    tile = lax.axis_index("tile")
    total_rows = lax.axis_size("tile") * rows

    def activate(hidden, layer):
        values = hidden.astype(jnp.float32)
        scale = lax.rsqrt(jnp.mean(values * values, axis=-1, keepdims=True) + 1e-06)
        half = values * scale * (0.5 * gain_ref[layer : layer + 1, :])
        return half * (1.0 + jnp.tanh(half))

    @pl.loop(0, rows + 4)
    def _(row):
        at = pl.ds(pl.multiple_of(row * cols, 16), cols)
        stacked = x_ref[at, :]
        for frame in range(frames):
            hidden = jnp.dot(
                stacked, w_ref[frame], preferred_element_type=jnp.float32
            ).astype(jnp.bfloat16)
            h0[frame, at, :] = hidden
            a1[frame, at, :] = activate(hidden, 0).astype(jnp.bfloat16)

    in_group = lax.broadcasted_iota(jnp.int32, (BLK, BLK), 0) // 32
    out_group = lax.broadcasted_iota(jnp.int32, (BLK, BLK), 1) // 32
    diagonal = (in_group == out_group).astype(jnp.float32).astype(jnp.bfloat16)
    size = CHUNK * cols
    column = lax.rem(lax.broadcasted_iota(jnp.int32, (size, BLK), 0), cols)

    def conv(layer, source, base, first_frame, row_count, target):
        @pl.loop(0, 2)
        def _(half):
            lanes = pl.ds(pl.multiple_of(half * BLK, BLK), BLK)

            @pl.loop(0, 9)
            def _(tap):
                for dx in range(3):
                    narrow = cw_ref[layer, tap * 3 + dx, :, lanes]
                    wide = jnp.concatenate([narrow] * (BLK // 32), axis=0)
                    wexp[dx, pl.ds(pl.multiple_of(tap * BLK, BLK), BLK), :] = wide * diagonal

            def one_frame(frame, taps):
                @pl.loop(0, row_count // CHUNK)
                def _(chunk):
                    start = chunk * size
                    pieces = [
                        source[
                            frame + dt - 2,
                            pl.ds(pl.multiple_of(start + dy * cols, 16), size),
                            lanes,
                        ]
                        for dt in range(3 - taps, 3)
                        for dy in range(3)
                    ]
                    joined = jnp.concatenate(pieces, axis=1)
                    total = base[
                        frame, pl.ds(pl.multiple_of(start + cols, 16), size), lanes
                    ].astype(jnp.float32)
                    for dx in range(3):
                        term = jnp.dot(
                            joined,
                            wexp[dx, (3 - taps) * 3 * BLK :, :],
                            preferred_element_type=jnp.float32,
                        )
                        if dx == 0:
                            term = jnp.where(column == 0, 0.0, pltpu.roll(term, 1, 0))
                        if dx == 2:
                            term = jnp.where(
                                column == cols - 1, 0.0, pltpu.roll(term, size - 1, 0)
                            )
                        total = total + term
                    target[
                        frame - first_frame, pl.ds(pl.multiple_of(start, 16), size), lanes
                    ] = total.astype(jnp.bfloat16)

            for frame in range(first_frame, min(2, frames)):
                one_frame(frame, frame + 1)
            pl.loop(2, frames)(lambda frame: one_frame(frame, 3))

    conv(0, a1, h0, 0, rows + 2, h1)

    @pl.loop(0, rows + 2)
    def _(row):
        place = tile * rows + row - 1
        keep = ((place >= 0) & (place < total_rows)).astype(jnp.float32)
        at = pl.ds(pl.multiple_of(row * cols, 16), cols)
        for frame in range(frames):
            a2[frame, at, :] = (activate(h1[frame, at, :], 1) * keep).astype(jnp.bfloat16)

    conv(1, a2, h1, CTX, rows, h0)

    for frame in range(frames - CTX):
        out_ref[frame] = jnp.dot(
            h0[frame, : rows * cols, :], head_ref[...], preferred_element_type=jnp.float32
        ).astype(jnp.bfloat16)


def shards(
    clean_latents,
    noise_draws,
    noise_level,
    memory_bank,
    memory_index,
    stem_weight,
    memory_weight,
    conv_weight,
    norm_gain,
    head_weight,
):
    latent, channels = stem_weight.shape
    frames, rows, merged = clean_latents.shape[1:]
    cols = merged // latent
    sigma = noise_level[0]
    noisy = (
        (clean_latents[0].astype(jnp.float32) + sigma * noise_draws[0].astype(jnp.float32))
        * lax.rsqrt(1.0 + sigma * sigma)
    ).astype(jnp.bfloat16)
    previous = shifted(clean_latents[0, frames - CTX :], "span", 1)
    memory = fetch_memory(memory_bank, memory_index)
    stack = jnp.concatenate([memory, previous, noisy], axis=0)
    stack = with_halo(stack, (("tile", 1),), 2)
    depth = stack.shape[0] * latent
    wide = rows + 4
    stack = jnp.transpose(
        stack.reshape(stack.shape[0], wide, cols, latent), (1, 2, 0, 3)
    ).reshape(wide * cols, depth)
    count = CTX + frames
    weights = jnp.concatenate(
        [
            jnp.broadcast_to(memory_weight[None], (count,) + memory_weight.shape),
            (
                jnp.eye(count, dtype=jnp.bfloat16)[:, :, None, None] * stem_weight[None, None]
            ).reshape(count, count * latent, channels),
        ],
        axis=1,
    )
    taps = conv_weight.reshape(conv_weight.shape[0], 27, conv_weight.shape[4], channels)
    vmem = pl.BlockSpec(memory_space=pltpu.VMEM)
    output = pl.pallas_call(
        functools.partial(kernel, rows),
        out_shape=jax.ShapeDtypeStruct((frames, rows * cols, latent), jnp.bfloat16),
        in_specs=[vmem] * 5,
        out_specs=vmem,
        scratch_shapes=[
            pltpu.VMEM((count, wide * cols, channels), jnp.bfloat16),
            pltpu.VMEM((count, wide * cols, channels), jnp.bfloat16),
            pltpu.VMEM((count, (rows + 2) * cols, channels), jnp.bfloat16),
            pltpu.VMEM((count, (rows + 2) * cols, channels), jnp.bfloat16),
            pltpu.VMEM((3, 9 * BLK, BLK), jnp.bfloat16),
        ],
        compiler_params=pltpu.CompilerParams(vmem_limit_bytes=56 * 2**20),
    )(stack, weights, taps, norm_gain, head_weight)
    return output.reshape(1, frames, rows, merged)


def solution(mesh):
    return jax.shard_map(
        shards,
        mesh=mesh,
        in_specs=(
            P("span", None, "tile", None),
            P("span", None, "tile", None),
            P("span"),
            P("span", "tile", None),
            P("span", None),
            P(),
            P(),
            P(),
            P(),
            P(),
        ),
        out_specs=P("span", None, "tile", None),
        check_vma=False,
    )
```

```python
import functools

import jax
import jax.numpy as jnp
from jax import lax
from jax.experimental import pallas as pl
from jax.experimental.pallas import tpu as pltpu
from jax.sharding import PartitionSpec as P

CTX = 2
CAP = 4
BLK = 256
CHUNK1 = 6
CHUNK2 = 4


def shifted(value, axis, steps):
    count = lax.axis_size(axis)
    first, last = (max(0, -steps), min(count, count - steps))
    return lax.ppermute(value, axis, [(source, source + steps) for source in range(first, last)])


def with_halo(block, sides, width):
    for axis, dim in sides:
        count = lax.axis_size(axis)
        forward = [(i, i + 1) for i in range(count - 1)]
        backward = [(target, source) for source, target in forward]
        low = lax.ppermute(
            lax.slice_in_dim(block, block.shape[dim] - width, None, axis=dim), axis, forward
        )
        high = lax.ppermute(lax.slice_in_dim(block, 0, width, axis=dim), axis, backward)
        block = jnp.concatenate([low, block, high], axis=dim)
    return block


def select_frames(frames, index):
    chosen = index[:, None] == jnp.arange(frames.shape[0], dtype=jnp.int32)[None, :]
    return jnp.einsum(
        "sf,frm->srm",
        chosen.astype(jnp.bfloat16),
        frames,
        preferred_element_type=jnp.float32,
    ).astype(jnp.bfloat16)


def fetch_memory(memory_bank, memory_index):
    wanted = memory_index[0]
    bank_frames, row_count, merged = memory_bank.shape
    span_count = lax.axis_size("span")
    memory_count = wanted.shape[0]
    owner_span = wanted // bank_frames
    local_frame = wanted % bank_frames
    positions = jnp.arange(memory_count, dtype=jnp.int32)
    same_owner = (owner_span[:, None] == owner_span[None, :]) & (
        positions[None, :] < positions[:, None]
    )
    owner_rank = jnp.sum(same_owner.astype(jnp.int32), axis=1)
    reply_slot = owner_span * CAP + owner_rank
    slot_match = jnp.arange(span_count * CAP, dtype=jnp.int32)[:, None] == reply_slot[None, :]
    request = jnp.sum(jnp.where(slot_match, local_frame[None, :] + 1, 0), axis=1) - 1
    request = request.reshape(span_count, CAP)
    incoming = lax.all_to_all(request, "span", split_axis=0, concat_axis=0, tiled=True)
    picked = select_frames(memory_bank, incoming.reshape(-1)).reshape(
        span_count, CAP, row_count, merged
    )
    returned = lax.all_to_all(picked, "span", split_axis=0, concat_axis=0, tiled=True)
    return select_frames(returned.reshape(span_count * CAP, row_count, merged), reply_slot)


def kernel(
    rows, x_ref, stem_ref, mem_ref, cw_ref, gain_ref, head_ref, out_ref, hf, wt, h0, a1, h1, a2, wexp
):
    frames = h0.shape[0]
    latent = stem_ref.shape[0]
    spread = 128 // latent
    mems = x_ref.shape[0] - frames
    cols = x_ref.shape[1] // (rows + 4) * spread
    tile = lax.axis_index("tile")
    total_rows = lax.axis_size("tile") * rows

    def activate(hidden, layer):
        values = hidden.astype(jnp.float32)
        scale = lax.rsqrt(jnp.mean(values * values, axis=-1, keepdims=True) + 1e-06)
        half = values * scale * (0.5 * gain_ref[layer : layer + 1, :])
        return half * (1.0 + jnp.tanh(half))

    for member in range(mems):
        narrow = mem_ref[member * latent : (member + 1) * latent, :]
        wt[member * 128 : (member + 1) * 128, :] = jnp.concatenate([narrow] * spread, axis=0)
    stem = jnp.concatenate([stem_ref[...]] * spread, axis=0)
    chunks = x_ref.shape[1]
    lane_column = lax.broadcasted_iota(jnp.int32, (16, 128), 1) // latent
    for place in range(spread):
        mask = (lane_column == place).astype(jnp.float32).astype(jnp.bfloat16)[:1]
        stacked = jnp.concatenate([x_ref[member] * mask for member in range(mems)], axis=1)
        memory_term = jnp.dot(stacked, wt[...], preferred_element_type=jnp.float32)
        for frame in range(frames):
            term = memory_term + jnp.dot(
                x_ref[mems + frame] * mask, stem, preferred_element_type=jnp.float32
            )
            for lane in range(term.shape[1] // 128):
                hf[frame, lane, pl.ds(place, chunks, stride=spread), :] = term[
                    :, lane * 128 : (lane + 1) * 128
                ]

    @pl.loop(0, rows + 4)
    def _(row):
        at = pl.ds(pl.multiple_of(row * cols, 16), cols)
        for frame in range(frames):
            hidden = jnp.concatenate(
                [hf[frame, lane, at, :] for lane in range(hf.shape[1])], axis=1
            ).astype(jnp.bfloat16)
            h0[frame, at, :] = hidden
            a1[frame, at, :] = activate(hidden, 0).astype(jnp.bfloat16)

    in_group = lax.broadcasted_iota(jnp.int32, (BLK, BLK), 0) // 32
    out_group = lax.broadcasted_iota(jnp.int32, (BLK, BLK), 1) // 32
    diagonal = (in_group == out_group).astype(jnp.float32).astype(jnp.bfloat16)
    def conv(layer, source, base, first_frame, row_count, target, chunk_rows):
        size = chunk_rows * cols
        column = lax.rem(lax.broadcasted_iota(jnp.int32, (size, BLK), 0), cols)

        @pl.loop(0, 2)
        def _(half):
            lanes = pl.ds(pl.multiple_of(half * BLK, BLK), BLK)

            @pl.loop(0, 9)
            def _(tap):
                for dx in range(3):
                    narrow = cw_ref[layer, tap * 3 + dx, :, lanes]
                    wide = jnp.concatenate([narrow] * (BLK // 32), axis=0)
                    wexp[dx, pl.ds(pl.multiple_of(tap * BLK, BLK), BLK), :] = wide * diagonal

            def one_frame(frame, taps):
                @pl.loop(0, row_count // chunk_rows)
                def _(chunk):
                    start = chunk * size
                    pieces = [
                        source[
                            frame + dt - 2,
                            pl.ds(pl.multiple_of(start + dy * cols, 16), size),
                            lanes,
                        ]
                        for dt in range(3 - taps, 3)
                        for dy in range(3)
                    ]
                    joined = jnp.concatenate(pieces, axis=1)
                    total = base[
                        frame, pl.ds(pl.multiple_of(start + cols, 16), size), lanes
                    ].astype(jnp.float32)
                    for dx in range(3):
                        term = jnp.dot(
                            joined,
                            wexp[dx, (3 - taps) * 3 * BLK :, :],
                            preferred_element_type=jnp.float32,
                        )
                        if dx == 0:
                            term = jnp.where(column == 0, 0.0, pltpu.roll(term, 1, 0))
                        if dx == 2:
                            term = jnp.where(
                                column == cols - 1, 0.0, pltpu.roll(term, size - 1, 0)
                            )
                        total = total + term
                    target[
                        frame - first_frame, pl.ds(pl.multiple_of(start, 16), size), lanes
                    ] = total.astype(jnp.bfloat16)

            for frame in range(first_frame, min(2, frames)):
                one_frame(frame, frame + 1)
            pl.loop(2, frames)(lambda frame: one_frame(frame, 3))

    conv(0, a1, h0, 0, rows + 2, h1, CHUNK1 if (rows + 2) % CHUNK1 == 0 else 1)

    @pl.loop(0, rows + 2)
    def _(row):
        place = tile * rows + row - 1
        keep = ((place >= 0) & (place < total_rows)).astype(jnp.float32)
        at = pl.ds(pl.multiple_of(row * cols, 16), cols)
        for frame in range(frames):
            a2[frame, at, :] = (activate(h1[frame, at, :], 1) * keep).astype(jnp.bfloat16)

    conv(1, a2, h1, CTX, rows, h0, CHUNK2 if rows % CHUNK2 == 0 else 1)

    for frame in range(frames - CTX):
        out_ref[frame] = jnp.dot(
            h0[frame, : rows * cols, :], head_ref[...], preferred_element_type=jnp.float32
        ).astype(jnp.bfloat16)


def shards(
    clean_latents,
    noise_draws,
    noise_level,
    memory_bank,
    memory_index,
    stem_weight,
    memory_weight,
    conv_weight,
    norm_gain,
    head_weight,
):
    latent, channels = stem_weight.shape
    frames, rows, merged = clean_latents.shape[1:]
    cols = merged // latent
    sigma = noise_level[0]
    noisy = (
        (clean_latents[0].astype(jnp.float32) + sigma * noise_draws[0].astype(jnp.float32))
        * lax.rsqrt(1.0 + sigma * sigma)
    ).astype(jnp.bfloat16)
    previous = shifted(clean_latents[0, frames - CTX :], "span", 1)
    memory = fetch_memory(memory_bank, memory_index)
    stack = jnp.concatenate([memory, previous, noisy], axis=0)
    stack = with_halo(stack, (("tile", 1),), 2)
    wide = rows + 4
    count = CTX + frames
    stack = stack.reshape(stack.shape[0], wide * merged // 128, 128)
    taps = conv_weight.reshape(conv_weight.shape[0], 27, conv_weight.shape[4], channels)
    vmem = pl.BlockSpec(memory_space=pltpu.VMEM)
    output = pl.pallas_call(
        functools.partial(kernel, rows),
        out_shape=jax.ShapeDtypeStruct((frames, rows * cols, latent), jnp.bfloat16),
        in_specs=[vmem] * 6,
        out_specs=vmem,
        scratch_shapes=[
            pltpu.VMEM((count, channels // 128, wide * cols, 128), jnp.float32),
            pltpu.VMEM((memory.shape[0] * 128, channels), jnp.bfloat16),
            pltpu.VMEM((count, wide * cols, channels), jnp.bfloat16),
            pltpu.VMEM((count, wide * cols, channels), jnp.bfloat16),
            pltpu.VMEM((count, (rows + 2) * cols, channels), jnp.bfloat16),
            pltpu.VMEM((count, (rows + 2) * cols, channels), jnp.bfloat16),
            pltpu.VMEM((3, 9 * BLK, BLK), jnp.bfloat16),
        ],
        compiler_params=pltpu.CompilerParams(vmem_limit_bytes=56 * 2**20),
    )(stack, stem_weight, memory_weight, taps, norm_gain, head_weight)
    return output.reshape(1, frames, rows, merged)


def solution(mesh):
    return jax.shard_map(
        shards,
        mesh=mesh,
        in_specs=(
            P("span", None, "tile", None),
            P("span", None, "tile", None),
            P("span"),
            P("span", "tile", None),
            P("span", None),
            P(),
            P(),
            P(),
            P(),
            P(),
        ),
        out_specs=P("span", None, "tile", None),
        check_vma=False,
    )
```

```python
import functools

import jax
import jax.numpy as jnp
from jax import lax
from jax.experimental import pallas as pl
from jax.experimental.pallas import tpu as pltpu
from jax.sharding import PartitionSpec as P

CTX = 2
CAP = 4
BLK = 256
CHUNK1 = 6
CHUNK2 = 4


def shifted(value, axis, steps):
    count = lax.axis_size(axis)
    first, last = (max(0, -steps), min(count, count - steps))
    return lax.ppermute(value, axis, [(source, source + steps) for source in range(first, last)])


def with_halo(block, sides, width):
    for axis, dim in sides:
        count = lax.axis_size(axis)
        forward = [(i, i + 1) for i in range(count - 1)]
        backward = [(target, source) for source, target in forward]
        low = lax.ppermute(
            lax.slice_in_dim(block, block.shape[dim] - width, None, axis=dim), axis, forward
        )
        high = lax.ppermute(lax.slice_in_dim(block, 0, width, axis=dim), axis, backward)
        block = jnp.concatenate([low, block, high], axis=dim)
    return block


def select_frames(frames, index):
    chosen = index[:, None] == jnp.arange(frames.shape[0], dtype=jnp.int32)[None, :]
    return jnp.einsum(
        "sf,frm->srm",
        chosen.astype(jnp.bfloat16),
        frames,
        preferred_element_type=jnp.float32,
    ).astype(jnp.bfloat16)


def fetch_memory(memory_bank, memory_index):
    wanted = memory_index[0]
    bank_frames, row_count, merged = memory_bank.shape
    span_count = lax.axis_size("span")
    memory_count = wanted.shape[0]
    owner_span = wanted // bank_frames
    local_frame = wanted % bank_frames
    positions = jnp.arange(memory_count, dtype=jnp.int32)
    same_owner = (owner_span[:, None] == owner_span[None, :]) & (
        positions[None, :] < positions[:, None]
    )
    owner_rank = jnp.sum(same_owner.astype(jnp.int32), axis=1)
    reply_slot = owner_span * CAP + owner_rank
    slot_match = jnp.arange(span_count * CAP, dtype=jnp.int32)[:, None] == reply_slot[None, :]
    request = jnp.sum(jnp.where(slot_match, local_frame[None, :] + 1, 0), axis=1) - 1
    request = request.reshape(span_count, CAP)
    incoming = lax.all_to_all(request, "span", split_axis=0, concat_axis=0, tiled=True)
    picked = select_frames(memory_bank, incoming.reshape(-1)).reshape(
        span_count, CAP, row_count, merged
    )
    returned = lax.all_to_all(picked, "span", split_axis=0, concat_axis=0, tiled=True)
    return select_frames(returned.reshape(span_count * CAP, row_count, merged), reply_slot)


def kernel(
    rows, x_ref, stem_ref, mem_ref, cw_ref, gain_ref, head_ref, out_ref, hf, wt, h0, a1, h1, a2, wexp
):
    frames = h0.shape[0]
    latent = stem_ref.shape[0]
    spread = 128 // latent
    mems = x_ref.shape[0] - frames
    cols = x_ref.shape[1] // (rows + 4) * spread
    tile = lax.axis_index("tile")
    total_rows = lax.axis_size("tile") * rows

    def activate(hidden, layer):
        values = hidden.astype(jnp.float32)
        scale = lax.rsqrt(jnp.mean(values * values, axis=-1, keepdims=True) + 1e-06)
        half = values * scale * (0.5 * gain_ref[layer : layer + 1, :])
        return half * (1.0 + jnp.tanh(half))

    for member in range(mems):
        narrow = mem_ref[member * latent : (member + 1) * latent, :]
        wt[member * 128 : (member + 1) * 128, :] = jnp.concatenate([narrow] * spread, axis=0)
    stem = jnp.concatenate([stem_ref[...]] * spread, axis=0)
    chunks = x_ref.shape[1]
    lane_column = lax.broadcasted_iota(jnp.int32, (16, 128), 1) // latent
    for place in range(spread):
        mask = (lane_column == place).astype(jnp.float32).astype(jnp.bfloat16)[:1]
        stacked = jnp.concatenate([x_ref[member] * mask for member in range(mems)], axis=1)
        memory_term = jnp.dot(stacked, wt[...], preferred_element_type=jnp.float32)
        for frame in range(frames):
            term = memory_term + jnp.dot(
                x_ref[mems + frame] * mask, stem, preferred_element_type=jnp.float32
            )
            for lane in range(term.shape[1] // 128):
                hf[frame, lane, pl.ds(place, chunks, stride=spread), :] = term[
                    :, lane * 128 : (lane + 1) * 128
                ]

    @pl.loop(0, rows + 4)
    def _(row):
        at = pl.ds(pl.multiple_of(row * cols, 16), cols)
        for frame in range(frames):
            hidden = jnp.concatenate(
                [hf[frame, lane, at, :] for lane in range(hf.shape[1])], axis=1
            ).astype(jnp.bfloat16)
            h0[frame, at, :] = hidden
            a1[frame, at, :] = activate(hidden, 0).astype(jnp.bfloat16)

    in_group = lax.broadcasted_iota(jnp.int32, (BLK, BLK), 0) // 32
    out_group = lax.broadcasted_iota(jnp.int32, (BLK, BLK), 1) // 32
    diagonal = (in_group == out_group).astype(jnp.float32).astype(jnp.bfloat16)
    def conv(layer, source, base, first_frame, row_count, target, chunk_rows):
        size = chunk_rows * cols
        column = lax.rem(lax.broadcasted_iota(jnp.int32, (size, BLK), 0), cols)

        @pl.loop(0, 2)
        def _(half):
            lanes = pl.ds(pl.multiple_of(half * BLK, BLK), BLK)

            @pl.loop(0, 9)
            def _(tap):
                for dx in range(3):
                    narrow = cw_ref[layer, tap * 3 + dx, :, lanes]
                    wide = jnp.concatenate([narrow] * (BLK // 32), axis=0)
                    wexp[dx, pl.ds(pl.multiple_of(tap * BLK, BLK), BLK), :] = wide * diagonal

            def one_frame(frame, taps):
                def one_chunk(chunk):
                    start = chunk * size
                    pieces = [
                        source[
                            frame + dt - 2,
                            pl.ds(start + dy * cols, size),
                            lanes,
                        ]
                        for dt in range(3 - taps, 3)
                        for dy in range(3)
                    ]
                    joined = jnp.concatenate(pieces, axis=1)
                    total = base[
                        frame, pl.ds(start + cols, size), lanes
                    ].astype(jnp.float32)
                    for dx in range(3):
                        term = jnp.dot(
                            joined,
                            wexp[dx, (3 - taps) * 3 * BLK :, :],
                            preferred_element_type=jnp.float32,
                        )
                        if dx == 0:
                            term = jnp.where(column == 0, 0.0, pltpu.roll(term, 1, 0))
                        if dx == 2:
                            term = jnp.where(
                                column == cols - 1, 0.0, pltpu.roll(term, size - 1, 0)
                            )
                        total = total + term
                    target[
                        frame - first_frame, pl.ds(start, size), lanes
                    ] = total.astype(jnp.bfloat16)

                for chunk in range(row_count // chunk_rows):
                    one_chunk(chunk)

            for frame in range(first_frame, frames):
                one_frame(frame, min(frame + 1, 3))

    conv(0, a1, h0, 0, rows + 2, h1, CHUNK1 if (rows + 2) % CHUNK1 == 0 else 1)

    @pl.loop(0, rows + 2)
    def _(row):
        place = tile * rows + row - 1
        keep = ((place >= 0) & (place < total_rows)).astype(jnp.float32)
        at = pl.ds(pl.multiple_of(row * cols, 16), cols)
        for frame in range(frames):
            a2[frame, at, :] = (activate(h1[frame, at, :], 1) * keep).astype(jnp.bfloat16)

    conv(1, a2, h1, CTX, rows, h0, CHUNK2 if rows % CHUNK2 == 0 else 1)

    for frame in range(frames - CTX):
        out_ref[frame] = jnp.dot(
            h0[frame, : rows * cols, :], head_ref[...], preferred_element_type=jnp.float32
        ).astype(jnp.bfloat16)


def shards(
    clean_latents,
    noise_draws,
    noise_level,
    memory_bank,
    memory_index,
    stem_weight,
    memory_weight,
    conv_weight,
    norm_gain,
    head_weight,
):
    latent, channels = stem_weight.shape
    frames, rows, merged = clean_latents.shape[1:]
    cols = merged // latent
    sigma = noise_level[0]
    noisy = (
        (clean_latents[0].astype(jnp.float32) + sigma * noise_draws[0].astype(jnp.float32))
        * lax.rsqrt(1.0 + sigma * sigma)
    ).astype(jnp.bfloat16)
    previous = shifted(clean_latents[0, frames - CTX :], "span", 1)
    memory = fetch_memory(with_halo(memory_bank, (("tile", 1),), 2), memory_index)
    sequence = with_halo(jnp.concatenate([previous, noisy], axis=0), (("tile", 1),), 2)
    stack = jnp.concatenate([memory, sequence], axis=0)
    wide = rows + 4
    count = CTX + frames
    stack = stack.reshape(stack.shape[0], wide * merged // 128, 128)
    taps = conv_weight.reshape(conv_weight.shape[0], 27, conv_weight.shape[4], channels)
    vmem = pl.BlockSpec(memory_space=pltpu.VMEM)
    output = pl.pallas_call(
        functools.partial(kernel, rows),
        out_shape=jax.ShapeDtypeStruct((frames, rows * cols, latent), jnp.bfloat16),
        in_specs=[vmem] * 6,
        out_specs=vmem,
        scratch_shapes=[
            pltpu.VMEM((count, channels // 128, wide * cols, 128), jnp.float32),
            pltpu.VMEM((memory.shape[0] * 128, channels), jnp.bfloat16),
            pltpu.VMEM((count, wide * cols, channels), jnp.bfloat16),
            pltpu.VMEM((count, wide * cols, channels), jnp.bfloat16),
            pltpu.VMEM((count, (rows + 2) * cols, channels), jnp.bfloat16),
            pltpu.VMEM((count, (rows + 2) * cols, channels), jnp.bfloat16),
            pltpu.VMEM((3, 9 * BLK, BLK), jnp.bfloat16),
        ],
        compiler_params=pltpu.CompilerParams(vmem_limit_bytes=56 * 2**20),
    )(stack, stem_weight, memory_weight, taps, norm_gain, head_weight)
    return output.reshape(1, frames, rows, merged)


def solution(mesh):
    return jax.shard_map(
        shards,
        mesh=mesh,
        in_specs=(
            P("span", None, "tile", None),
            P("span", None, "tile", None),
            P("span"),
            P("span", "tile", None),
            P("span", None),
            P(),
            P(),
            P(),
            P(),
            P(),
        ),
        out_specs=P("span", None, "tile", None),
        check_vma=False,
    )
```
